32 devices in a mesh: rows: 8 (over z, core), cols: 4 (over y, x).
Axes of the slice: x: 2, y: 2, z: 4, core: 2. Of those that a mesh axis runs over, the one named last changes fastest.
Arguments:
- source_points: float32 [32, 16384], P(None, ('rows', 'cols')), may hold values from -3.5 to 3.5
- target_points: float32 [32, 8192], P(None, ('cols', 'rows')), may hold values from -3.5 to 3.5
- target_init: float32 [8192], P('cols'), may hold values from -3 to 3
Outputs:
- source_potential: float32 [16384], P('rows')
- target_potential: float32 [8192], P('cols')
The draws below stay inside these ranges and needn't reach their ends.
All inputs are finite; a program needn't handle non-finite values.
Results may differ from the reference program's by a relative error of at most 0.0003.
Values sent between devices are 32-bit elements; how exact they have to be, the bound alone decides.
No kernel may reach another device: no remote copies, remote signals or barrier semaphores. Data moves between devices by JAX's collectives and lax.ppermute only.
A program may use at most 64 MiB of HBM per device.

```python
import math
import jax
import jax.numpy as jnp
from jax import lax

K = 32
ITERS = 4
NSRC = 16384
NTGT = 8192


def spread_points(key, count):
    return 0.18 * jnp.clip(jax.random.normal(key, (K, count), jnp.float32), -4.0, 4.0)


def draw_source_points(key, part):
    key = jax.random.fold_in(key, 11)
    return spread_points(key, NSRC)


def draw_target_points(key, part):
    key = jax.random.fold_in(key, 23)
    return spread_points(key, NTGT)


def steps_of(rng, extent, pieces, least, high):
    def one(dim, blocks):
        draws = jax.random.uniform(jax.random.fold_in(jax.random.fold_in(rng, 6), dim), (blocks,), jnp.float32, least / len(pieces), high / len(pieces))
        return jnp.repeat(jnp.exp(draws), extent[dim] // blocks).reshape((-1,) + (1,) * (len(extent) - dim - 1))

    gain = one(*pieces[0])
    for cut in pieces[1:]:
        gain = gain * one(*cut)
    return gain


def noise(key, shape, spread, limit, shards=(), dtype=jnp.bfloat16):
    drawn = jax.random.normal(key, shape, jnp.float32) * spread
    if len(shards) > 0:
        drawn = steps_of(key, shape, shards, -0.22, 0.18) * drawn
    return jnp.clip(drawn, min=-limit, max=limit).astype(dtype)


def setup_inputs(seed: int = 0) -> dict:
    splits = jax.random.split(jax.random.key(seed), 4)
    source_points = draw_source_points(jax.random.fold_in(splits[3], 71), 0)
    target_points = draw_target_points(jax.random.fold_in(splits[3], 71), 0)
    target_init = noise(splits[2], (NTGT,), 0.5, 3.0, ((0, 4),), jnp.float32)
    return {"source_points": source_points, "target_points": target_points, "target_init": target_init}


eps = 0.2


def cost_block(left, right):
    cross = lax.dot_general(left, right, (((0,), (0,)), ((), ())), precision=lax.Precision.HIGHEST, preferred_element_type=jnp.float32)
    sq_left = jnp.sum(left * left, axis=0)
    sq_right = jnp.sum(right * right, axis=0)
    return sq_left[:, None] + sq_right[None, :] - 2.0 * cross


def blocked(points, width):
    count = points.shape[1]
    return points.reshape(points.shape[0], count // width, width).transpose(1, 0, 2)


def reference(source_points, target_points, target_init):
    nsrc = source_points.shape[1]
    ntgt = target_points.shape[1]
    wide_src = math.gcd(nsrc, 1024)
    wide_tgt = math.gcd(ntgt, 1024)
    src_blocks = blocked(source_points, wide_src)
    tgt_blocks = blocked(target_points, wide_tgt)
    potential_g = target_init.astype(jnp.float32)
    potential_f = jnp.zeros((nsrc,), jnp.float32)
    for step in range(ITERS):
        def row_step(block):
            scores = (potential_g[None, :] - cost_block(block, target_points)) / eps
            peak = jnp.max(scores, axis=1)
            total = jnp.sum(jnp.exp(scores - peak[:, None]), axis=1)
            return eps * math.log(ntgt) - eps * (peak + jnp.log(total))

        potential_f = lax.map(row_step, src_blocks).reshape(-1)

        def col_step(block):
            scores = (potential_f[:, None] - cost_block(source_points, block)) / eps
            peak = jnp.max(scores, axis=0)
            total = jnp.sum(jnp.exp(scores - peak[None, :]), axis=0)
            return eps * math.log(nsrc) - eps * (peak + jnp.log(total))

        potential_g = lax.map(col_step, tgt_blocks).reshape(-1)
    return potential_f, potential_g
```

```python
import functools
import math

import jax
import jax.numpy as jnp
from jax import lax
from jax.experimental import pallas as pl
from jax.experimental.pallas import tpu as pltpu
from jax.sharding import PartitionSpec as P

ITERS = 4
EPS = 0.2
ALPHA = math.log2(math.e) / EPS
LANES = 128
SUB = 8
MIB = 1024 * 1024
TILE = 256
LIFT = 50.0

VMEM = pl.BlockSpec(memory_space=pltpu.VMEM)
HBM = pl.BlockSpec(memory_space=pltpu.HBM)
SMEM = pl.BlockSpec(memory_space=pltpu.SMEM)


def tree(op, items):
    items = list(items)
    while len(items) > 1:
        items = [op(*items[k : k + 2]) if k + 1 < len(items) else items[k] for k in range(0, len(items), 2)]
    return items[0]


def lse2(parts):
    peak = tree(jnp.maximum, parts)
    return peak + jnp.log2(tree(jnp.add, [jnp.exp2(part - peak) for part in parts]))


def split3(value):
    high = value.astype(jnp.bfloat16)
    rest = value - high.astype(jnp.float32)
    mid = rest.astype(jnp.bfloat16)
    low = (rest - mid.astype(jnp.float32)).astype(jnp.bfloat16)
    return high, mid, low


def store_rows(ref, row):
    for k in range(row.shape[1] // LANES):
        ref[k : k + 1, :] = row[:, k * LANES : (k + 1) * LANES]


def set_addend(right, first, cols, row):
    high, mid, low = (part.astype(jnp.float32) for part in split3(row))
    index = lax.broadcasted_iota(jnp.int32, (2 * SUB, row.shape[1]), 0)
    rows = jnp.where(index < 3, 1.0, 0.0)
    for k, part in enumerate((high, mid, low)):
        rows = jnp.where(index == 3 + k, part, rows)
    right[first : first + 2 * SUB, cols] = rows.astype(jnp.bfloat16)


def score_tile(left, right, c, t):
    return jnp.dot(
        left[c * TILE : (c + 1) * TILE, :],
        right[:, t * TILE : (t + 1) * TILE],
        preferred_element_type=jnp.float32,
    )


def fold_rows(op, tile):
    return tree(op, [tile[r * SUB : (r + 1) * SUB, :] for r in range(tile.shape[0] // SUB)])


def sweep(left, right, op, change, start, acc):
    width = min(TILE, right.shape[1])

    def step(n, _):
        c = n // (right.shape[1] // width)
        t = n % (right.shape[1] // width)
        cols = pl.ds(pl.multiple_of(t * width, width), width)
        rows = pl.ds(pl.multiple_of(c * TILE, TILE), TILE)
        tile = jnp.dot(left[rows, :], right[:, cols], preferred_element_type=jnp.float32)
        acc[:, cols] = op(acc[:, cols], fold_rows(op, change(tile)))
        return 0

    acc[...] = jnp.full(acc.shape, start, jnp.float32)
    lax.fori_loop(0, left.shape[0] // TILE * (right.shape[1] // width), step, 0)


def exact_lse(left, right, first, acc):
    every = slice(0, right.shape[1])
    set_addend(right, first, every, jnp.zeros((1, right.shape[1]), jnp.float32))
    sweep(left, right, jnp.maximum, lambda tile: tile, -jnp.inf, acc)
    peak = jnp.max(acc[...], axis=0, keepdims=True)
    set_addend(right, first, every, -peak)
    sweep(left, right, jnp.add, jnp.exp2, 0.0, acc)
    return peak + jnp.log2(jnp.sum(acc[...], axis=0, keepdims=True))


def place_sources(x, right, cols):
    depth, width = x.shape
    first = 6 * depth
    high, mid, low = split3(x * (2.0 * ALPHA))
    for k, part in enumerate((high, high, high, mid, mid, low)):
        right[k * depth : (k + 1) * depth, cols] = part
    right[first:, cols] = jnp.zeros((right.shape[0] - first, width), jnp.bfloat16)
    set_addend(right, first, cols, jnp.zeros((1, width), jnp.float32))


def put_rows(ref, start, row):
    for k in range(row.shape[1] // LANES):
        ref[pl.ds(start + k, 1), :] = row[:, k * LANES : (k + 1) * LANES]


def guarded_sums(left, right, first, pieces, lse):
    held = []
    for start, count, row in pieces:
        width = min(TILE, count)
        for t in range(count // width):
            cols = pl.ds(pl.multiple_of(start + t * width, LANES), width)
            held.append((cols, row + t * (width // LANES)))

    def tile(c, cols):
        return jnp.dot(left[c * TILE : (c + 1) * TILE, :], right[:, cols], preferred_element_type=jnp.float32)

    peaks = []
    for cols, _ in held:
        peak = jnp.max(fold_rows(jnp.maximum, tile(0, cols)), axis=0, keepdims=True)
        peaks.append(peak)
    for (cols, _), peak in zip(held, peaks):
        set_addend(right, first, cols, -peak)
    totals = []
    for cols, _ in held:
        total = None
        for c in range(left.shape[0] // TILE):
            part = fold_rows(jnp.add, jnp.exp2(tile(c, cols)))
            total = part if total is None else total + part
        totals.append(jnp.sum(total, axis=0, keepdims=True))
    for (_, row), peak, total in zip(held, peaks, totals):
        put_rows(lse, row, peak + jnp.log2(total))
    return jnp.max(tree(jnp.maximum, totals)) < 2.0**100


def place_pieces(points, index, pieces):
    width = pieces[0].shape[1]
    for distance, piece in enumerate(pieces):
        start = pl.multiple_of((index ^ distance) * width, LANES)
        points[:, pl.ds(start, width)] = piece[...]


def own_scores_kernel(place, own_tgt, own_g0, src, *refs):
    lse, norms, left, right, stack, points, acc, held_tgt, g0, sems = refs[-10:]
    tgt = refs[:-10]
    copies = [
        pltpu.make_async_copy(source, target, sems.at[k])
        for k, (source, target) in enumerate(((own_tgt, held_tgt), (own_g0, g0)))
    ]
    for copy in copies:
        copy.start()
    depth, width = src.shape
    first = 6 * depth
    x = src[...]
    store_rows(norms, jnp.sum(x * x, axis=0, keepdims=True))
    place_sources(x, right, slice(0, width))
    for copy in copies:
        copy.wait()

    place_pieces(points, place[1], (held_tgt, *tgt))
    ntgt = left.shape[0]
    y = points[...]
    gamma = ALPHA * (g0[...] - jnp.sum(y * y, axis=0, keepdims=True))
    high, mid, low = split3(y)
    for k, part in enumerate((high, mid, low, high, mid, high)):
        stack[k * depth : (k + 1) * depth, :] = part
    index = lax.broadcasted_iota(jnp.int32, (stack.shape[0] - first, ntgt), 0)
    rows = jnp.where((index >= 3) & (index < 6), 1.0, 0.0)
    for k, part in enumerate(split3(gamma)):
        rows = jnp.where(index == k, part.astype(jnp.float32), rows)
    stack[first:, :] = rows.astype(jnp.bfloat16)
    for c in range(ntgt // TILE):
        left[c * TILE : (c + 1) * TILE, :] = stack[:, c * TILE : (c + 1) * TILE].T

    fine = guarded_sums(left, right, first, [(0, width, 0)], lse)

    @pl.when(jnp.logical_not(fine))
    def _():
        store_rows(lse, exact_lse(left, right, first, acc))


def scores_kernel(place, left, own_right, own_lse, own_norms, *refs):
    lse, norms, right, acc = refs[-4:]
    src = refs[:-4]
    depth, width = src[0].shape
    first = 6 * depth
    own = place[0] * width
    right[:, pl.ds(pl.multiple_of(own, LANES), width)] = own_right[...]
    pieces = []
    for distance, piece in enumerate(src, 1):
        owner = place[0] ^ distance
        start = owner * width
        row = owner * (width // LANES)
        x = piece[...]
        put_rows(norms, row, jnp.sum(x * x, axis=0, keepdims=True))
        place_sources(x, right, pl.ds(pl.multiple_of(start, LANES), width))
        pieces.append((start, width, row))
    fine = guarded_sums(left, right, first, pieces, lse)

    @pl.when(jnp.logical_not(fine))
    def _():
        store_rows(lse, exact_lse(left, right, first, acc))

    for k in range(width // LANES):
        row = pl.ds(place[0] * (width // LANES) + k, 1)
        lse[row, :] = own_lse[k : k + 1, :]
        norms[row, :] = own_norms[k : k + 1, :]


def read_row(ref, k):
    return ref[k : k + 1, :]


QUARTER = LANES // 4


def lane_mask(index):
    return lax.broadcasted_iota(jnp.int32, (SUB, LANES), 1) == index


def group(index):
    return pl.ds(pl.multiple_of(index * SUB, SUB), SUB)


def join_chains(chains):
    lanes = lax.broadcasted_iota(jnp.int32, (SUB, LANES), 1)
    value = chains[-1]
    for k in reversed(range(len(chains) - 1)):
        value = jnp.where(lanes < (k + 1) * QUARTER, chains[k], value)
    return value


def fold_lanes(reduce, partial, out, wide=None):
    for h in range(out.shape[0] // SUB):
        chains = []
        for index in range(LANES):
            rows = slice((h * LANES + index) * SUB, (h * LANES + index + 1) * SUB)
            value = reduce(partial[rows, :], axis=1, keepdims=True)
            if wide is not None:
                wide[rows, :] = jnp.broadcast_to(value, (SUB, LANES))
            if index % QUARTER == 0:
                chains.append(jnp.broadcast_to(value, (SUB, LANES)))
            else:
                chains[-1] = jnp.where(lane_mask(index), value, chains[-1])
        out[h * SUB : (h + 1) * SUB, :] = join_chains(chains)


def first_columns_kernel(log_ntgt, first, left, _, row_lse, ratios, right, phi, peaks, lse, partial, wide, sums):
    phi[...] = log_ntgt - row_lse[...]
    for k in range(phi.shape[0]):
        set_addend(right, first, slice(k * LANES, (k + 1) * LANES), read_row(phi, k) + LIFT)
    halves = TILE // LANES
    for t in range(ratios.shape[1] // TILE):
        for c in range(ratios.shape[0] // TILE):
            rows = slice(c * TILE, (c + 1) * TILE)
            tile = jnp.exp2(score_tile(left, right, c, t))
            ratios[rows, t * TILE : (t + 1) * TILE] = tile
            part = tree(jnp.add, [tile[:, k * LANES : (k + 1) * LANES] for k in range(halves)])
            partial[rows, :] = part if t == 0 else partial[rows, :] + part
    fold_lanes(jnp.sum, partial, sums)
    peaks[...] = jnp.zeros(peaks.shape, jnp.float32)

    @pl.when(jnp.logical_not(jnp.min(sums[...]) >= 2.0**-20))
    def _():
        groups = ratios.shape[0] // SUB
        few = 4

        def score_step(n, _):
            c = n // (ratios.shape[1] // TILE)
            t = n % (ratios.shape[1] // TILE)
            cols = pl.ds(pl.multiple_of(t * TILE, TILE), TILE)
            rows = pl.ds(pl.multiple_of(c * TILE, TILE), TILE)
            ratios[rows, cols] = jnp.dot(left[rows, :], right[:, cols], preferred_element_type=jnp.float32)
            return 0

        def peak_step(c, _):
            for t in range(few):
                rows = group(c * few + t)
                partial[rows, :] = tree(
                    jnp.maximum, [ratios[rows, k * LANES : (k + 1) * LANES] for k in range(ratios.shape[1] // LANES)]
                )
            return 0

        def ratio_step(c, _):
            for t in range(few):
                rows = group(c * few + t)
                peak = wide[rows, :]
                tiles = [
                    jnp.exp2(ratios[rows, k * LANES : (k + 1) * LANES] - peak)
                    for k in range(ratios.shape[1] // LANES)
                ]
                for k, value in enumerate(tiles):
                    ratios[rows, k * LANES : (k + 1) * LANES] = value
                partial[rows, :] = tree(jnp.add, tiles)
            return 0

        lax.fori_loop(0, ratios.shape[0] // TILE * (ratios.shape[1] // TILE), score_step, 0)
        lax.fori_loop(0, groups // few, peak_step, 0)
        fold_lanes(jnp.max, partial, peaks, wide)
        lax.fori_loop(0, groups // few, ratio_step, 0)
        fold_lanes(jnp.sum, partial, sums)

    lse[...] = peaks[...] + (jnp.log2(sums[...]) - LIFT)


def row_sums(ratios, weights, out):
    count = ratios.shape[1]
    total = jnp.zeros((SUB, count), jnp.float32)
    for h in range(weights.shape[0] // SUB):
        held = weights[h * SUB : (h + 1) * SUB, :]
        for index in range(LANES):
            rows = slice((h * LANES + index) * SUB, (h * LANES + index + 1) * SUB)
            total = total + ratios[rows, :] * jnp.broadcast_to(held[:, index : index + 1], (SUB, count))
    store_rows(out, jnp.sum(total, axis=0, keepdims=True))


def first_rows_kernel(log_nsrc, ratios, peaks, col_lse, out, weights, base):
    shift = log_nsrc - col_lse[...]
    base[...] = shift
    weights[...] = jnp.exp2(peaks[...] + (shift - LIFT))
    row_sums(ratios, weights[...], out)


def rows_kernel(nsrc, ratios, weights, total, out):
    row_sums(ratios, weights[...] * (nsrc / total[...]), out)


def columns_kernel(ntgt, ratios, weights, total, out, scale):
    total = total[...]
    scale[...] = ntgt / total
    count = ratios.shape[1]
    tiles = count // LANES
    scales = jnp.concatenate([jnp.broadcast_to(read_row(scale, k), (SUB, LANES)) for k in range(tiles)], axis=1)
    for h in range(out.shape[0] // SUB):
        chains = []
        for index in range(LANES):
            rows = slice((h * LANES + index) * SUB, (h * LANES + index + 1) * SUB)
            value = jnp.sum(ratios[rows, :] * scales, axis=1, keepdims=True)
            if index % QUARTER == 0:
                chains.append(jnp.broadcast_to(value, (SUB, LANES)))
            else:
                chains[-1] = jnp.where(lane_mask(index), value, chains[-1])
        rows = slice(h * SUB, (h + 1) * SUB)
        out[rows, :] = join_chains(chains) * weights[rows, :]


def finish_kernel(log_nsrc, base, total, out):
    out[...] = (base[...] + (log_nsrc - jnp.log2(total[...]))) * (1.0 / ALPHA)


def swap(value, axis, distance):
    return lax.ppermute(value, axis, [(k, k ^ distance) for k in range(lax.axis_size(axis))])


def hop(value, distance, lead, step=1):
    nrows, ncols = lax.axis_size("rows"), lax.axis_size("cols")
    perm = []
    for row in range(nrows):
        for col in range(step - 1, ncols, step):
            other = col ^ distance
            perm.append((row * ncols + col, lead(row, col, other) * ncols + other))
    return lax.ppermute(value, ("rows", "cols"), perm)


def to_block(value, distance, odd=False):
    return hop(value, distance, lambda row, col, other: row ^ (other & 1), 1 + odd)


def same_block(value, distance):
    return hop(value, distance, lambda row, col, other: row ^ ((col ^ other) & 1))


def combine_cols(reduce, value):
    return reduce([value] + [same_block(value, d) for d in range(1, lax.axis_size("cols"))])


def combine_rows(reduce, value):
    value = reduce([value, swap(value, "rows", 1)])
    return reduce([value] + [swap(value, "rows", d) for d in range(3, lax.axis_size("rows"), 2)])


def add_all(values):
    return tree(jnp.add, values)


def gather_rows(value):
    far = {0: value}
    for d in range(3, lax.axis_size("rows"), 2):
        far[d] = swap(value, "rows", d)
    pieces = dict(far)
    for d, piece in far.items():
        pieces[d ^ 1] = swap(piece, "rows", 1)
    return [pieces[d] for d in range(1, lax.axis_size("rows"))]


def call(kernel, out_shape, nin, scratch=(), limit=8, aliases=None, smem=0, hbm=0):
    return pl.pallas_call(
        kernel,
        out_shape=out_shape,
        in_specs=[SMEM] * smem + [HBM] * hbm + [VMEM] * (nin - smem - hbm),
        out_specs=[VMEM] * len(out_shape),
        scratch_shapes=list(scratch),
        input_output_aliases=aliases or {},
        compiler_params=pltpu.CompilerParams(vmem_limit_bytes=limit * MIB),
    )


def body(source_points, target_points, target_init):
    ncols = lax.axis_size("cols")
    nrows = lax.axis_size("rows")
    depth = source_points.shape[0]
    src_count = source_points.shape[1] * ncols
    tgt_count = target_points.shape[1] * nrows
    nsrc = src_count * nrows
    ntgt = tgt_count * ncols
    log_nsrc = math.log2(nsrc)
    log_ntgt = math.log2(ntgt)
    stack = -(-(6 * depth + 2 * SUB) // LANES) * LANES
    f32 = jnp.float32
    by_src = jax.ShapeDtypeStruct((src_count // LANES, LANES), f32)
    by_tgt = jax.ShapeDtypeStruct((tgt_count // LANES, LANES), f32)
    square = pltpu.VMEM((tgt_count, src_count), f32)
    wide = pltpu.VMEM((tgt_count, LANES), f32)
    row_src = pltpu.VMEM(by_src.shape, f32)
    row_tgt = pltpu.VMEM(by_tgt.shape, f32)

    def pin(value):
        return pltpu.with_memory_space_constraint(value, pltpu.VMEM)

    targets = gather_rows(target_points)
    sources = [to_block(source_points, d) for d in range(ncols)]
    place = jnp.stack([lax.axis_index("cols"), lax.axis_index("rows")]).astype(jnp.int32)
    bf16 = jnp.bfloat16
    piece = source_points.shape[1]
    by_piece = jax.ShapeDtypeStruct((piece // LANES, LANES), f32)
    own_lse, own_norms, left, own_right = call(
        own_scores_kernel,
        [by_piece, by_piece, pltpu.VMEM((tgt_count, stack), bf16), pltpu.VMEM((stack, piece), bf16)],
        3 + nrows,
        [
            pltpu.VMEM((stack, tgt_count), bf16),
            pltpu.VMEM((depth, tgt_count), f32),
            pltpu.VMEM((SUB, piece), f32),
            pltpu.VMEM(target_points.shape, f32),
            pltpu.VMEM((1, tgt_count), f32),
            pltpu.SemaphoreType.DMA((2,)),
        ],
        limit=16,
        smem=1,
        hbm=2,
    )(
        place,
        *(
            pltpu.with_memory_space_constraint(own, pltpu.HBM)
            for own in (target_points, target_init.reshape(1, tgt_count))
        ),
        sources[0],
        *targets,
    )
    left = pin(left)
    lse, norms, right = call(
        scores_kernel,
        [by_src, by_src, pltpu.VMEM((stack, src_count), bf16)],
        4 + ncols,
        [pltpu.VMEM((SUB, src_count), f32)],
        limit=16,
        smem=1,
    )(place, left, pin(own_right), own_lse, own_norms, *sources[1:])
    ratios, _, phi, peaks, lse = call(
        functools.partial(first_columns_kernel, log_ntgt, 6 * depth),
        [square, pltpu.VMEM((stack, src_count), jnp.bfloat16), by_src, by_tgt, by_tgt],
        3,
        [wide, wide, row_tgt],
        aliases={1: 1},
    )(left, pin(right), combine_cols(lse2, lse))
    ratios = pin(ratios)
    total, weights, base = call(
        functools.partial(first_rows_kernel, log_nsrc),
        [by_src, by_tgt, by_tgt],
        3,
    )(ratios, peaks, combine_rows(lse2, lse))
    for step in range(1, ITERS):
        row_total = combine_cols(add_all, total)
        (total,) = call(
            functools.partial(columns_kernel, float(ntgt)),
            [by_tgt],
            3,
            [row_src],
        )(ratios, weights, row_total)
        if step == ITERS - 1:
            total, row_total = lax.optimization_barrier((total, row_total))
        total = combine_rows(add_all, total)
        if step < ITERS - 1:
            (total,) = call(
                functools.partial(rows_kernel, float(nsrc)),
                [by_src],
                3,
            )(ratios, weights, total)
    f = (phi + (log_ntgt - jnp.log2(row_total))) * (1.0 / ALPHA) + norms
    f = jnp.where(lax.axis_index("cols") % 2 == 1, to_block(f, 0, odd=True), f)
    (delta,) = call(functools.partial(finish_kernel, log_nsrc), [by_tgt], 2)(base, total)
    delta = delta.reshape(-1, SUB, LANES).transpose(0, 2, 1).reshape(-1)
    return f.reshape(-1), target_init + delta


def solution(mesh):
    in_specs = (P(None, ("rows", "cols")), P(None, ("cols", "rows")), P("cols"))
    out_specs = (P("rows"), P("cols"))
    return jax.shard_map(body, mesh=mesh, in_specs=in_specs, out_specs=out_specs, check_vma=False)
```

```python
import functools
import math

import jax
import jax.numpy as jnp
from jax import lax
from jax.experimental import pallas as pl
from jax.experimental.pallas import tpu as pltpu
from jax.sharding import PartitionSpec as P

ITERS = 4
EPS = 0.2
ALPHA = math.log2(math.e) / EPS
LANES = 128
SUB = 8
MIB = 1024 * 1024
TILE = 256
HEAD = 40.0
ROW_LOW, ROW_HIGH = 2.0**20, 2.0**80
SCALE_LOW, COLUMN_LOW = 2.0**-60, 2.0**-30

VMEM = pl.BlockSpec(memory_space=pltpu.VMEM)
HBM = pl.BlockSpec(memory_space=pltpu.HBM)
SMEM = pl.BlockSpec(memory_space=pltpu.SMEM)


def tree(op, items):
    items = list(items)
    while len(items) > 1:
        items = [op(*items[k : k + 2]) if k + 1 < len(items) else items[k] for k in range(0, len(items), 2)]
    return items[0]


def lse2(parts):
    peak = tree(jnp.maximum, parts)
    return peak + jnp.log2(tree(jnp.add, [jnp.exp2(part - peak) for part in parts]))


def split3(value):
    high = value.astype(jnp.bfloat16)
    rest = value - high.astype(jnp.float32)
    mid = rest.astype(jnp.bfloat16)
    low = (rest - mid.astype(jnp.float32)).astype(jnp.bfloat16)
    return high, mid, low


def store_rows(ref, row):
    for k in range(row.shape[1] // LANES):
        ref[k : k + 1, :] = row[:, k * LANES : (k + 1) * LANES]


def set_addend(right, first, cols, row):
    high, mid, low = (part.astype(jnp.float32) for part in split3(row))
    index = lax.broadcasted_iota(jnp.int32, (2 * SUB, row.shape[1]), 0)
    rows = jnp.where(index < 3, 1.0, 0.0)
    for k, part in enumerate((high, mid, low)):
        rows = jnp.where(index == 3 + k, part, rows)
    right[first : first + 2 * SUB, cols] = rows.astype(jnp.bfloat16)


def score_tile(left, right, c, t):
    return jnp.dot(
        left[c * TILE : (c + 1) * TILE, :],
        right[:, t * TILE : (t + 1) * TILE],
        preferred_element_type=jnp.float32,
    )


def fold_rows(op, tile):
    return tree(op, [tile[r * SUB : (r + 1) * SUB, :] for r in range(tile.shape[0] // SUB)])


def sweep(left, right, op, change, start, acc):
    width = min(TILE, right.shape[1])

    def step(n, _):
        c = n // (right.shape[1] // width)
        t = n % (right.shape[1] // width)
        cols = pl.ds(pl.multiple_of(t * width, width), width)
        rows = pl.ds(pl.multiple_of(c * TILE, TILE), TILE)
        tile = jnp.dot(left[rows, :], right[:, cols], preferred_element_type=jnp.float32)
        acc[:, cols] = op(acc[:, cols], fold_rows(op, change(tile)))
        return 0

    acc[...] = jnp.full(acc.shape, start, jnp.float32)
    lax.fori_loop(0, left.shape[0] // TILE * (right.shape[1] // width), step, 0)


def exact_lse(left, right, first, acc):
    every = slice(0, right.shape[1])
    set_addend(right, first, every, jnp.zeros((1, right.shape[1]), jnp.float32))
    sweep(left, right, jnp.maximum, lambda tile: tile, -jnp.inf, acc)
    peak = jnp.max(acc[...], axis=0, keepdims=True)
    set_addend(right, first, every, -peak)
    sweep(left, right, jnp.add, jnp.exp2, 0.0, acc)
    return peak + jnp.log2(jnp.sum(acc[...], axis=0, keepdims=True))


def place_sources(x, right, cols):
    depth, width = x.shape
    first = 6 * depth
    high, mid, low = split3(x * (2.0 * ALPHA))
    for k, part in enumerate((high, high, high, mid, mid, low)):
        right[k * depth : (k + 1) * depth, cols] = part
    right[first:, cols] = jnp.zeros((right.shape[0] - first, width), jnp.bfloat16)
    set_addend(right, first, cols, jnp.zeros((1, width), jnp.float32))


def put_rows(ref, start, row):
    for k in range(row.shape[1] // LANES):
        ref[pl.ds(start + k, 1), :] = row[:, k * LANES : (k + 1) * LANES]


def guarded_sums(left, right, pieces, base, lse, ratios):
    totals = []
    for start, place, count, row in pieces:
        width = min(TILE, count)
        for t in range(count // width):
            cols = pl.ds(pl.multiple_of(start + t * width, LANES), width)
            out = pl.ds(pl.multiple_of(place + t * width, LANES), width)
            total = None
            for c in range(left.shape[0] // TILE):
                rows = slice(c * TILE, (c + 1) * TILE)
                tile = jnp.exp2(jnp.dot(left[rows, :], right[:, cols], preferred_element_type=jnp.float32))
                ratios[rows, out] = tile
                part = fold_rows(jnp.add, tile)
                total = part if total is None else total + part
            total = jnp.sum(total, axis=0, keepdims=True)
            put_rows(lse, row + t * (width // LANES), base + jnp.log2(total))
            totals.append(total)
    low, high = tree(jnp.minimum, totals), tree(jnp.maximum, totals)
    return jnp.min(jnp.where((low > ROW_LOW) & (high < ROW_HIGH), 1.0, 0.0)) > 0.5


def place_pieces(points, index, pieces):
    width = pieces[0].shape[1]
    for distance, piece in enumerate(pieces):
        start = pl.multiple_of((index ^ distance) * width, LANES)
        points[:, pl.ds(start, width)] = piece[...]


def own_scores_kernel(place, own_src, own_tgt, own_g0, *refs):
    lse, norms, left, right, base, flag, ratios, stack, points, acc, held_src, held_tgt, g0, sems = refs[-14:]
    tgt = refs[:-14]
    copies = [
        pltpu.make_async_copy(source, target, sems.at[k])
        for k, (source, target) in enumerate(((own_src, held_src), (own_tgt, held_tgt), (own_g0, g0)))
    ]
    for copy in copies:
        copy.start()
    for copy in copies:
        copy.wait()
    depth, width = held_src.shape
    first = 6 * depth
    x = held_src[...]
    store_rows(norms, jnp.sum(x * x, axis=0, keepdims=True))
    place_sources(x, right, slice(0, width))

    place_pieces(points, place[1], (held_tgt, *tgt))
    ntgt = left.shape[0]
    y = points[...]
    gamma = ALPHA * (g0[...] - jnp.sum(y * y, axis=0, keepdims=True))
    top = jnp.max(gamma, axis=1, keepdims=True)
    base[...] = jnp.broadcast_to(top - HEAD, base.shape)
    gamma = gamma - top + HEAD
    high, mid, low = split3(y)
    for k, part in enumerate((high, mid, low, high, mid, high)):
        stack[k * depth : (k + 1) * depth, :] = part
    index = lax.broadcasted_iota(jnp.int32, (stack.shape[0] - first, ntgt), 0)
    rows = jnp.where((index >= 3) & (index < 6), 1.0, 0.0)
    for k, part in enumerate(split3(gamma)):
        rows = jnp.where(index == k, part.astype(jnp.float32), rows)
    stack[first:, :] = rows.astype(jnp.bfloat16)
    for c in range(ntgt // TILE):
        left[c * TILE : (c + 1) * TILE, :] = stack[:, c * TILE : (c + 1) * TILE].T

    fine = guarded_sums(left, right, [(0, place[0] * width, width, 0)], base[:, :1], lse, ratios)
    flag[...] = jnp.full(flag.shape, jnp.where(fine, 1.0, 0.0), jnp.float32)

    @pl.when(jnp.logical_not(fine))
    def _():
        store_rows(lse, exact_lse(left, right, first, acc) + base[:, :1])


def scores_kernel(place, left, own_right, own_lse, own_norms, base, own_flag, _, *refs):
    lse, norms, right, flag, ratios, acc = refs[-6:]
    src = refs[:-6]
    depth, width = src[0].shape
    first = 6 * depth
    own = place[0] * width
    right[:, pl.ds(pl.multiple_of(own, LANES), width)] = own_right[...]
    pieces = []
    for distance, piece in enumerate(src, 1):
        owner = place[0] ^ distance
        start = owner * width
        row = owner * (width // LANES)
        x = piece[...]
        put_rows(norms, row, jnp.sum(x * x, axis=0, keepdims=True))
        place_sources(x, right, pl.ds(pl.multiple_of(start, LANES), width))
        pieces.append((start, start, width, row))
    fine = guarded_sums(left, right, pieces, base[:, :1], lse, ratios)
    flag[...] = jnp.where(fine, own_flag[...], 0.0)

    @pl.when(jnp.logical_not(fine))
    def _():
        store_rows(lse, exact_lse(left, right, first, acc) + base[:, :1])

    for k in range(width // LANES):
        row = pl.ds(place[0] * (width // LANES) + k, 1)
        lse[row, :] = own_lse[k : k + 1, :]
        norms[row, :] = own_norms[k : k + 1, :]


def read_row(ref, k):
    return ref[k : k + 1, :]


QUARTER = LANES // 4


def lane_mask(index):
    return lax.broadcasted_iota(jnp.int32, (SUB, LANES), 1) == index


def group(index):
    return pl.ds(pl.multiple_of(index * SUB, SUB), SUB)


def join_chains(chains):
    lanes = lax.broadcasted_iota(jnp.int32, (SUB, LANES), 1)
    value = chains[-1]
    for k in reversed(range(len(chains) - 1)):
        value = jnp.where(lanes < (k + 1) * QUARTER, chains[k], value)
    return value


def fold_lanes(reduce, partial, out, wide=None):
    for h in range(out.shape[0] // SUB):
        chains = []
        for index in range(LANES):
            rows = slice((h * LANES + index) * SUB, (h * LANES + index + 1) * SUB)
            value = reduce(partial[rows, :], axis=1, keepdims=True)
            if wide is not None:
                wide[rows, :] = jnp.broadcast_to(value, (SUB, LANES))
            if index % QUARTER == 0:
                chains.append(jnp.broadcast_to(value, (SUB, LANES)))
            else:
                chains[-1] = jnp.where(lane_mask(index), value, chains[-1])
        out[h * SUB : (h + 1) * SUB, :] = join_chains(chains)


def column_sums(ratios, scale, out):
    tiles = ratios.shape[1] // LANES
    scales = jnp.concatenate([jnp.broadcast_to(read_row(scale, k), (SUB, LANES)) for k in range(tiles)], axis=1)
    for h in range(out.shape[0] // SUB):
        chains = []
        for index in range(LANES):
            rows = slice((h * LANES + index) * SUB, (h * LANES + index + 1) * SUB)
            value = jnp.sum(ratios[rows, :] * scales, axis=1, keepdims=True)
            if index % QUARTER == 0:
                chains.append(jnp.broadcast_to(value, (SUB, LANES)))
            else:
                chains[-1] = jnp.where(lane_mask(index), value, chains[-1])
        out[h * SUB : (h + 1) * SUB, :] = join_chains(chains)


def first_columns_kernel(
    log_ntgt, first, left, base, flag, row_lse, _, __, ratios, right, phi, scale, peaks, lse, partial, wide, sums
):
    phi[...] = log_ntgt - row_lse[...]
    scale[...] = jnp.exp2(phi[...] + base[...])
    column_sums(ratios, scale, sums)
    peaks[...] = jnp.zeros(peaks.shape, jnp.float32)
    low = jnp.min(jnp.where(flag[...] > 0.5, sums[...], -1.0))

    @pl.when(jnp.logical_not((low >= COLUMN_LOW) & (jnp.min(scale[...]) >= SCALE_LOW)))
    def _():
        for k in range(phi.shape[0]):
            set_addend(right, first, slice(k * LANES, (k + 1) * LANES), read_row(phi, k) + base[...])
        scale[...] = jnp.ones(scale.shape, jnp.float32)
        groups = ratios.shape[0] // SUB
        few = 4

        def score_step(n, _):
            c = n // (ratios.shape[1] // TILE)
            t = n % (ratios.shape[1] // TILE)
            cols = pl.ds(pl.multiple_of(t * TILE, TILE), TILE)
            rows = pl.ds(pl.multiple_of(c * TILE, TILE), TILE)
            ratios[rows, cols] = jnp.dot(left[rows, :], right[:, cols], preferred_element_type=jnp.float32)
            return 0

        def peak_step(c, _):
            for t in range(few):
                rows = group(c * few + t)
                partial[rows, :] = tree(
                    jnp.maximum, [ratios[rows, k * LANES : (k + 1) * LANES] for k in range(ratios.shape[1] // LANES)]
                )
            return 0

        def ratio_step(c, _):
            for t in range(few):
                rows = group(c * few + t)
                peak = wide[rows, :]
                tiles = [
                    jnp.exp2(ratios[rows, k * LANES : (k + 1) * LANES] - peak)
                    for k in range(ratios.shape[1] // LANES)
                ]
                for k, value in enumerate(tiles):
                    ratios[rows, k * LANES : (k + 1) * LANES] = value
                partial[rows, :] = tree(jnp.add, tiles)
            return 0

        lax.fori_loop(0, ratios.shape[0] // TILE * (ratios.shape[1] // TILE), score_step, 0)
        lax.fori_loop(0, groups // few, peak_step, 0)
        fold_lanes(jnp.max, partial, peaks, wide)
        lax.fori_loop(0, groups // few, ratio_step, 0)
        fold_lanes(jnp.sum, partial, sums)

    lse[...] = peaks[...] + jnp.log2(sums[...])


def row_sums(ratios, weights, scale, out):
    count = ratios.shape[1]
    total = jnp.zeros((SUB, count), jnp.float32)
    for h in range(weights.shape[0] // SUB):
        held = weights[h * SUB : (h + 1) * SUB, :]
        for index in range(LANES):
            rows = slice((h * LANES + index) * SUB, (h * LANES + index + 1) * SUB)
            total = total + ratios[rows, :] * jnp.broadcast_to(held[:, index : index + 1], (SUB, count))
    store_rows(out, jnp.sum(total, axis=0, keepdims=True))
    out[...] = out[...] * scale[...]


def first_rows_kernel(log_nsrc, ratios, scale, peaks, col_lse, out, weights, shift):
    shift[...] = log_nsrc - col_lse[...]
    weights[...] = jnp.exp2(peaks[...] + shift[...])
    row_sums(ratios, weights[...], scale, out)


def rows_kernel(nsrc, ratios, scale, weights, total, out):
    row_sums(ratios, weights[...] * (nsrc / total[...]), scale, out)


def columns_kernel(ntgt, ratios, scale, weights, total, out, held):
    held[...] = scale[...] * (ntgt / total[...])
    column_sums(ratios, held, out)
    out[...] = out[...] * weights[...]


def finish_kernel(log_nsrc, shift, total, out):
    out[...] = (shift[...] + (log_nsrc - jnp.log2(total[...]))) * (1.0 / ALPHA)


def swap(value, axis, distance):
    return lax.ppermute(value, axis, [(k, k ^ distance) for k in range(lax.axis_size(axis))])


def same_block(value, distance):
    nrows, ncols = lax.axis_size("rows"), lax.axis_size("cols")
    perm = [
        (row * ncols + col, (row ^ (distance & 1)) * ncols + (col ^ distance))
        for row in range(nrows)
        for col in range(ncols)
    ]
    return lax.ppermute(value, ("rows", "cols"), perm)


def combine_cols(reduce, value):
    return reduce([value] + [same_block(value, d) for d in range(1, lax.axis_size("cols"))])


def add_cores(reduce, value):
    return reduce([value, swap(value, "rows", 1)])


def combine_chips(reduce, value):
    return reduce([value] + [swap(value, "rows", d) for d in range(3, lax.axis_size("rows"), 2)])


def combine_rows(reduce, value):
    return combine_chips(reduce, add_cores(reduce, value))


def add_all(values):
    return tree(jnp.add, values)


def gather_rows(value):
    far = {0: value}
    for d in range(3, lax.axis_size("rows"), 2):
        far[d] = swap(value, "rows", d)
    pieces = dict(far)
    for d, piece in far.items():
        pieces[d ^ 1] = swap(piece, "rows", 1)
    return [pieces[d] for d in range(1, lax.axis_size("rows"))]


def call(kernel, out_shape, nin, scratch=(), limit=8, aliases=None, smem=0, hbm=0):
    return pl.pallas_call(
        kernel,
        out_shape=out_shape,
        in_specs=[SMEM] * smem + [HBM] * hbm + [VMEM] * (nin - smem - hbm),
        out_specs=[VMEM] * len(out_shape),
        scratch_shapes=list(scratch),
        input_output_aliases=aliases or {},
        compiler_params=pltpu.CompilerParams(vmem_limit_bytes=limit * MIB),
    )


def body(source_points, target_points, target_init):
    ncols = lax.axis_size("cols")
    nrows = lax.axis_size("rows")
    depth = source_points.shape[0]
    src_count = source_points.shape[1] * ncols
    tgt_count = target_points.shape[1] * nrows
    nsrc = src_count * nrows
    ntgt = tgt_count * ncols
    log_nsrc = math.log2(nsrc)
    log_ntgt = math.log2(ntgt)
    stack = -(-(6 * depth + 2 * SUB) // LANES) * LANES
    f32 = jnp.float32
    by_src = jax.ShapeDtypeStruct((src_count // LANES, LANES), f32)
    by_tgt = jax.ShapeDtypeStruct((tgt_count // LANES, LANES), f32)
    square = pltpu.VMEM((tgt_count, src_count), f32)
    wide = pltpu.VMEM((tgt_count, LANES), f32)
    row_src = pltpu.VMEM(by_src.shape, f32)
    row_tgt = pltpu.VMEM(by_tgt.shape, f32)

    def pin(value):
        return pltpu.with_memory_space_constraint(value, pltpu.VMEM)

    targets = gather_rows(target_points)
    sources = [same_block(source_points, d) for d in range(1, ncols)]
    place = jnp.stack([lax.axis_index("cols"), lax.axis_index("rows")]).astype(jnp.int32)
    bf16 = jnp.bfloat16
    piece = source_points.shape[1]
    by_piece = jax.ShapeDtypeStruct((piece // LANES, LANES), f32)
    line = jax.ShapeDtypeStruct((1, LANES), f32)
    own_lse, own_norms, left, own_right, base, own_flag, ratios = call(
        own_scores_kernel,
        [
            by_piece,
            by_piece,
            pltpu.VMEM((tgt_count, stack), bf16),
            pltpu.VMEM((stack, piece), bf16),
            line,
            line,
            square,
        ],
        3 + nrows,
        [
            pltpu.VMEM((stack, tgt_count), bf16),
            pltpu.VMEM((depth, tgt_count), f32),
            pltpu.VMEM((SUB, piece), f32),
            pltpu.VMEM(source_points.shape, f32),
            pltpu.VMEM(target_points.shape, f32),
            pltpu.VMEM((1, tgt_count), f32),
            pltpu.SemaphoreType.DMA((3,)),
        ],
        limit=16,
        smem=1,
        hbm=3,
    )(
        place,
        *(
            pltpu.with_memory_space_constraint(own, pltpu.HBM)
            for own in (source_points, target_points, target_init.reshape(1, tgt_count))
        ),
        *targets,
    )
    left = pin(left)
    lse, norms, right, flag, ratios = call(
        scores_kernel,
        [by_src, by_src, pltpu.VMEM((stack, src_count), bf16), line, square],
        7 + ncols,
        [pltpu.VMEM((SUB, src_count), f32)],
        limit=16,
        smem=1,
        aliases={7: 4},
    )(place, left, pin(own_right), own_lse, own_norms, base, own_flag, pin(ratios), *sources)
    ratios, _, phi, scale, peaks, lse = call(
        functools.partial(first_columns_kernel, log_ntgt, 6 * depth),
        [square, pltpu.VMEM((stack, src_count), bf16), by_src, by_src, by_tgt, by_tgt],
        6,
        [wide, wide, row_tgt],
        aliases={4: 0, 5: 1},
    )(left, base, flag, combine_cols(lse2, lse), pin(ratios), pin(right))
    ratios = pin(ratios)
    total, weights, shift = call(
        functools.partial(first_rows_kernel, log_nsrc),
        [by_src, by_tgt, by_tgt],
        4,
    )(ratios, scale, peaks, combine_rows(lse2, lse))
    for step in range(1, ITERS):
        row_total = combine_cols(add_all, total)
        (total,) = call(
            functools.partial(columns_kernel, float(ntgt)),
            [by_tgt],
            4,
            [row_src],
        )(ratios, scale, weights, row_total)
        total = add_cores(add_all, total)
        if step == ITERS - 1:
            total, row_total = lax.optimization_barrier((total, row_total))
        total = combine_chips(add_all, total)
        if step < ITERS - 1:
            (total,) = call(
                functools.partial(rows_kernel, float(nsrc)),
                [by_src],
                4,
            )(ratios, scale, weights, total)
    f = (phi + (log_ntgt - jnp.log2(row_total))) * (1.0 / ALPHA) + norms
    column = lax.broadcasted_iota(jnp.int32, f.shape, 0) // (piece // LANES)
    f = jnp.where((column - lax.axis_index("cols")) % 2 == 0, f, swap(f, "rows", 1))
    (delta,) = call(functools.partial(finish_kernel, log_nsrc), [by_tgt], 2)(shift, total)
    delta = delta.reshape(-1, SUB, LANES).transpose(0, 2, 1).reshape(-1)
    return f.reshape(-1), target_init + delta


def solution(mesh):
    in_specs = (P(None, ("rows", "cols")), P(None, ("cols", "rows")), P("cols"))
    out_specs = (P("rows"), P("cols"))
    return jax.shard_map(body, mesh=mesh, in_specs=in_specs, out_specs=out_specs, check_vma=False)
```

```python
import functools
import math

import jax
import jax.numpy as jnp
from jax import lax
from jax.experimental import pallas as pl
from jax.experimental.pallas import tpu as pltpu
from jax.sharding import PartitionSpec as P

ITERS = 4
EPS = 0.2
ALPHA = math.log2(math.e) / EPS
LANES = 128
SUB = 8
MIB = 1024 * 1024
TILE = 256
DEEP = 512
HEAD = 40.0
ROW_LOW, ROW_HIGH = 2.0**20, 2.0**80
SCALE_LOW, COLUMN_LOW = 2.0**-60, 2.0**-30

VMEM = pl.BlockSpec(memory_space=pltpu.VMEM)
HBM = pl.BlockSpec(memory_space=pltpu.HBM)
SMEM = pl.BlockSpec(memory_space=pltpu.SMEM)


def tree(op, items):
    items = list(items)
    while len(items) > 1:
        items = [op(*items[k : k + 2]) if k + 1 < len(items) else items[k] for k in range(0, len(items), 2)]
    return items[0]


def lse2(parts):
    peak = tree(jnp.maximum, parts)
    return peak + jnp.log2(tree(jnp.add, [jnp.exp2(part - peak) for part in parts]))


def split3(value):
    high = value.astype(jnp.bfloat16)
    rest = value - high.astype(jnp.float32)
    mid = rest.astype(jnp.bfloat16)
    low = (rest - mid.astype(jnp.float32)).astype(jnp.bfloat16)
    return high, mid, low


def store_rows(ref, row):
    for k in range(row.shape[1] // LANES):
        ref[k : k + 1, :] = row[:, k * LANES : (k + 1) * LANES]


def set_addend(right, first, cols, row):
    high, mid, low = (part.astype(jnp.float32) for part in split3(row))
    index = lax.broadcasted_iota(jnp.int32, (2 * SUB, row.shape[1]), 0)
    rows = jnp.where(index < 3, 1.0, 0.0)
    for k, part in enumerate((high, mid, low)):
        rows = jnp.where(index == 3 + k, part, rows)
    right[first : first + 2 * SUB, cols] = rows.astype(jnp.bfloat16)


def score_tile(left, right, c, t):
    return jnp.dot(
        left[c * TILE : (c + 1) * TILE, :],
        right[:, t * TILE : (t + 1) * TILE],
        preferred_element_type=jnp.float32,
    )


def fold_rows(op, tile):
    return tree(op, [tile[r * SUB : (r + 1) * SUB, :] for r in range(tile.shape[0] // SUB)])


def sweep(left, right, op, change, start, acc):
    width = min(TILE, right.shape[1])

    def step(n, _):
        c = n // (right.shape[1] // width)
        t = n % (right.shape[1] // width)
        cols = pl.ds(pl.multiple_of(t * width, width), width)
        rows = pl.ds(pl.multiple_of(c * TILE, TILE), TILE)
        tile = jnp.dot(left[rows, :], right[:, cols], preferred_element_type=jnp.float32)
        acc[:, cols] = op(acc[:, cols], fold_rows(op, change(tile)))
        return 0

    acc[...] = jnp.full(acc.shape, start, jnp.float32)
    lax.fori_loop(0, left.shape[0] // TILE * (right.shape[1] // width), step, 0)


def exact_lse(left, right, first, acc):
    every = slice(0, right.shape[1])
    set_addend(right, first, every, jnp.zeros((1, right.shape[1]), jnp.float32))
    sweep(left, right, jnp.maximum, lambda tile: tile, -jnp.inf, acc)
    peak = jnp.max(acc[...], axis=0, keepdims=True)
    set_addend(right, first, every, -peak)
    sweep(left, right, jnp.add, jnp.exp2, 0.0, acc)
    return peak + jnp.log2(jnp.sum(acc[...], axis=0, keepdims=True))


def place_sources(x, right, cols):
    depth, width = x.shape
    first = 6 * depth
    high, mid, low = split3(x * (2.0 * ALPHA))
    for k, part in enumerate((high, high, high, mid, mid, low)):
        right[k * depth : (k + 1) * depth, cols] = part
    right[first:, cols] = jnp.zeros((right.shape[0] - first, width), jnp.bfloat16)
    set_addend(right, first, cols, jnp.zeros((1, width), jnp.float32))


def put_rows(ref, start, row):
    for k in range(row.shape[1] // LANES):
        ref[pl.ds(start + k, 1), :] = row[:, k * LANES : (k + 1) * LANES]


def guarded_sums(left, right, pieces, base, lse, ratios):
    totals = []
    for start, place, count, row in pieces:
        width = min(TILE, count)
        for t in range(count // width):
            cols = pl.ds(pl.multiple_of(start + t * width, LANES), width)
            out = pl.ds(pl.multiple_of(place + t * width, LANES), width)
            total = None
            for c in range(left.shape[0] // DEEP):
                rows = slice(c * DEEP, (c + 1) * DEEP)
                tile = jnp.exp2(jnp.dot(left[rows, :], right[:, cols], preferred_element_type=jnp.float32))
                ratios[rows, out] = tile
                part = fold_rows(jnp.add, tile)
                total = part if total is None else total + part
            total = jnp.sum(total, axis=0, keepdims=True)
            put_rows(lse, row + t * (width // LANES), base + jnp.log2(total))
            totals.append(total)
    low, high = tree(jnp.minimum, totals), tree(jnp.maximum, totals)
    return jnp.min(jnp.where((low > ROW_LOW) & (high < ROW_HIGH), 1.0, 0.0)) > 0.5


def place_pieces(points, index, pieces):
    width = pieces[0].shape[1]
    for distance, piece in enumerate(pieces):
        start = pl.multiple_of((index ^ distance) * width, LANES)
        points[:, pl.ds(start, width)] = piece[...]


def own_pieces_kernel(own_src, own_tgt, own_g0, norms, right, tgt, g0, held_src, sems):
    copies = [
        pltpu.make_async_copy(source, target, sems.at[k])
        for k, (source, target) in enumerate(((own_src, held_src), (own_tgt, tgt), (own_g0, g0)))
    ]
    for copy in copies:
        copy.start()
    for copy in copies:
        copy.wait()
    x = held_src[...]
    store_rows(norms, jnp.sum(x * x, axis=0, keepdims=True))
    place_sources(x, right, slice(0, x.shape[1]))


def own_scores_kernel(place, own_right, g0, *refs):
    lse, left, right, base, flag, ratios, stack, points, acc = refs[-9:]
    tgt = refs[:-9]
    depth = tgt[0].shape[0]
    first = 6 * depth
    width = right.shape[1]

    place_pieces(points, place[1], tgt)
    ntgt = left.shape[0]
    y = points[...]
    gamma = ALPHA * (g0[...] - jnp.sum(y * y, axis=0, keepdims=True))
    top = jnp.max(gamma, axis=1, keepdims=True)
    base[...] = jnp.broadcast_to(top - HEAD, base.shape)
    gamma = gamma - top + HEAD
    high, mid, low = split3(y)
    for k, part in enumerate((high, mid, low, high, mid, high)):
        stack[k * depth : (k + 1) * depth, :] = part
    index = lax.broadcasted_iota(jnp.int32, (stack.shape[0] - first, ntgt), 0)
    rows = jnp.where((index >= 3) & (index < 6), 1.0, 0.0)
    for k, part in enumerate(split3(gamma)):
        rows = jnp.where(index == k, part.astype(jnp.float32), rows)
    stack[first:, :] = rows.astype(jnp.bfloat16)
    for c in range(ntgt // TILE):
        left[c * TILE : (c + 1) * TILE, :] = stack[:, c * TILE : (c + 1) * TILE].T

    fine = guarded_sums(left, own_right, [(0, place[0] * width, width, 0)], base[:, :1], lse, ratios)
    right[...] = own_right[...]
    flag[...] = jnp.full(flag.shape, jnp.where(fine, 1.0, 0.0), jnp.float32)

    @pl.when(jnp.logical_not(fine))
    def _():
        store_rows(lse, exact_lse(left, right, first, acc) + base[:, :1])


def scores_kernel(place, left, own_right, own_lse, own_norms, base, own_flag, _, *refs):
    lse, norms, right, flag, ratios, acc = refs[-6:]
    src = refs[:-6]
    depth, width = src[0].shape
    first = 6 * depth
    own = place[0] * width
    right[:, pl.ds(pl.multiple_of(own, LANES), width)] = own_right[...]
    pieces = []
    for distance, piece in enumerate(src, 1):
        owner = place[0] ^ distance
        start = owner * width
        row = owner * (width // LANES)
        x = piece[...]
        put_rows(norms, row, jnp.sum(x * x, axis=0, keepdims=True))
        place_sources(x, right, pl.ds(pl.multiple_of(start, LANES), width))
        pieces.append((start, start, width, row))
    fine = guarded_sums(left, right, pieces, base[:, :1], lse, ratios)
    flag[...] = jnp.where(fine, own_flag[...], 0.0)

    @pl.when(jnp.logical_not(fine))
    def _():
        store_rows(lse, exact_lse(left, right, first, acc) + base[:, :1])

    for k in range(width // LANES):
        row = pl.ds(place[0] * (width // LANES) + k, 1)
        lse[row, :] = own_lse[k : k + 1, :]
        norms[row, :] = own_norms[k : k + 1, :]


def read_row(ref, k):
    return ref[k : k + 1, :]


QUARTER = LANES // 4


def lane_mask(index):
    return lax.broadcasted_iota(jnp.int32, (SUB, LANES), 1) == index


def group(index):
    return pl.ds(pl.multiple_of(index * SUB, SUB), SUB)


def join_chains(chains):
    lanes = lax.broadcasted_iota(jnp.int32, (SUB, LANES), 1)
    value = chains[-1]
    for k in reversed(range(len(chains) - 1)):
        value = jnp.where(lanes < (k + 1) * QUARTER, chains[k], value)
    return value


def fold_lanes(reduce, partial, out, wide=None):
    for h in range(out.shape[0] // SUB):
        chains = []
        for index in range(LANES):
            rows = slice((h * LANES + index) * SUB, (h * LANES + index + 1) * SUB)
            value = reduce(partial[rows, :], axis=1, keepdims=True)
            if wide is not None:
                wide[rows, :] = jnp.broadcast_to(value, (SUB, LANES))
            if index % QUARTER == 0:
                chains.append(jnp.broadcast_to(value, (SUB, LANES)))
            else:
                chains[-1] = jnp.where(lane_mask(index), value, chains[-1])
        out[h * SUB : (h + 1) * SUB, :] = join_chains(chains)


def column_sums(ratios, scale, out):
    tiles = ratios.shape[1] // LANES
    scales = jnp.concatenate([jnp.broadcast_to(read_row(scale, k), (SUB, LANES)) for k in range(tiles)], axis=1)
    for h in range(out.shape[0] // SUB):
        chains = []
        for index in range(LANES):
            rows = slice((h * LANES + index) * SUB, (h * LANES + index + 1) * SUB)
            value = jnp.sum(ratios[rows, :] * scales, axis=1, keepdims=True)
            if index % QUARTER == 0:
                chains.append(jnp.broadcast_to(value, (SUB, LANES)))
            else:
                chains[-1] = jnp.where(lane_mask(index), value, chains[-1])
        out[h * SUB : (h + 1) * SUB, :] = join_chains(chains)


def first_columns_kernel(
    log_ntgt, first, left, base, flag, row_lse, _, __, ratios, right, phi, scale, peaks, lse, partial, wide, sums
):
    phi[...] = log_ntgt - row_lse[...]
    scale[...] = jnp.exp2(phi[...] + base[...])
    column_sums(ratios, scale, sums)
    peaks[...] = jnp.zeros(peaks.shape, jnp.float32)
    low = jnp.min(jnp.where(flag[...] > 0.5, sums[...], -1.0))

    @pl.when(jnp.logical_not((low >= COLUMN_LOW) & (jnp.min(scale[...]) >= SCALE_LOW)))
    def _():
        for k in range(phi.shape[0]):
            set_addend(right, first, slice(k * LANES, (k + 1) * LANES), read_row(phi, k) + base[...])
        scale[...] = jnp.ones(scale.shape, jnp.float32)
        groups = ratios.shape[0] // SUB
        few = 4

        def score_step(n, _):
            c = n // (ratios.shape[1] // TILE)
            t = n % (ratios.shape[1] // TILE)
            cols = pl.ds(pl.multiple_of(t * TILE, TILE), TILE)
            rows = pl.ds(pl.multiple_of(c * TILE, TILE), TILE)
            ratios[rows, cols] = jnp.dot(left[rows, :], right[:, cols], preferred_element_type=jnp.float32)
            return 0

        def peak_step(c, _):
            for t in range(few):
                rows = group(c * few + t)
                partial[rows, :] = tree(
                    jnp.maximum, [ratios[rows, k * LANES : (k + 1) * LANES] for k in range(ratios.shape[1] // LANES)]
                )
            return 0

        def ratio_step(c, _):
            for t in range(few):
                rows = group(c * few + t)
                peak = wide[rows, :]
                tiles = [
                    jnp.exp2(ratios[rows, k * LANES : (k + 1) * LANES] - peak)
                    for k in range(ratios.shape[1] // LANES)
                ]
                for k, value in enumerate(tiles):
                    ratios[rows, k * LANES : (k + 1) * LANES] = value
                partial[rows, :] = tree(jnp.add, tiles)
            return 0

        lax.fori_loop(0, ratios.shape[0] // TILE * (ratios.shape[1] // TILE), score_step, 0)
        lax.fori_loop(0, groups // few, peak_step, 0)
        fold_lanes(jnp.max, partial, peaks, wide)
        lax.fori_loop(0, groups // few, ratio_step, 0)
        fold_lanes(jnp.sum, partial, sums)

    lse[...] = peaks[...] + jnp.log2(sums[...])


def row_sums(ratios, weights, scale, out):
    count = ratios.shape[1]
    total = jnp.zeros((SUB, count), jnp.float32)
    for h in range(weights.shape[0] // SUB):
        held = weights[h * SUB : (h + 1) * SUB, :]
        for index in range(LANES):
            rows = slice((h * LANES + index) * SUB, (h * LANES + index + 1) * SUB)
            total = total + ratios[rows, :] * jnp.broadcast_to(held[:, index : index + 1], (SUB, count))
    store_rows(out, jnp.sum(total, axis=0, keepdims=True))
    out[...] = out[...] * scale[...]


def first_rows_kernel(log_nsrc, ratios, scale, peaks, col_lse, out, weights, shift):
    shift[...] = log_nsrc - col_lse[...]
    weights[...] = jnp.exp2(peaks[...] + shift[...])
    row_sums(ratios, weights[...], scale, out)


def rows_kernel(nsrc, ratios, scale, weights, total, out):
    row_sums(ratios, weights[...] * (nsrc / total[...]), scale, out)


def columns_kernel(ntgt, ratios, scale, weights, total, out, held):
    held[...] = scale[...] * (ntgt / total[...])
    column_sums(ratios, held, out)
    out[...] = out[...] * weights[...]


def finish_kernel(log_nsrc, shift, total, out):
    out[...] = (shift[...] + (log_nsrc - jnp.log2(total[...]))) * (1.0 / ALPHA)


def swap(value, axis, distance):
    return lax.ppermute(value, axis, [(k, k ^ distance) for k in range(lax.axis_size(axis))])


def parity(value):
    return sum((value >> k) & 1 for k in range(lax.axis_size("cols").bit_length())) % 2


def same_block(value, distance):
    nrows, ncols = lax.axis_size("rows"), lax.axis_size("cols")
    perm = [
        (row * ncols + col, (row ^ parity(distance)) * ncols + (col ^ distance))
        for row in range(nrows)
        for col in range(ncols)
    ]
    return lax.ppermute(value, ("rows", "cols"), perm)


def fold_ends(reduce, values):
    first = lax.optimization_barrier(reduce([values[0], values[-1]]))
    values = [first] + [reduce([values[-1 - k], values[k]]) for k in range(1, len(values) // 2)]
    while len(values) > 1:
        values = [reduce([values[k], values[-1 - k]]) for k in range(len(values) // 2)]
    return values[0]


def combine_cols(reduce, value):
    return fold_ends(reduce, [value] + [same_block(value, d) for d in range(1, lax.axis_size("cols"))])


def add_cores(reduce, value):
    return reduce([value, swap(value, "rows", 1)])


def combine_chips(reduce, value):
    return fold_ends(reduce, [value] + [swap(value, "rows", d) for d in range(3, lax.axis_size("rows"), 2)])


def combine_rows(reduce, value):
    return combine_chips(reduce, add_cores(reduce, value))


def add_all(values):
    return tree(jnp.add, values)


def gather_rows(value):
    count = lax.axis_size("rows")
    pieces = {1: swap(value, "rows", 1)}
    for d in range(3, count, 2):
        pieces[d] = swap(value, "rows", d)
    pieces[3], pieces[1] = lax.optimization_barrier((pieces[3], pieces[1]))
    for d in range(3, count, 2):
        pieces[d ^ 1] = swap(pieces[d], "rows", 1)
    return [pieces[d] for d in range(1, count)]


def call(kernel, out_shape, nin, scratch=(), limit=8, aliases=None, smem=0, hbm=0):
    return pl.pallas_call(
        kernel,
        out_shape=out_shape,
        in_specs=[SMEM] * smem + [HBM] * hbm + [VMEM] * (nin - smem - hbm),
        out_specs=[VMEM] * len(out_shape),
        scratch_shapes=list(scratch),
        input_output_aliases=aliases or {},
        compiler_params=pltpu.CompilerParams(vmem_limit_bytes=limit * MIB),
    )


def body(source_points, target_points, target_init):
    ncols = lax.axis_size("cols")
    nrows = lax.axis_size("rows")
    depth = source_points.shape[0]
    src_count = source_points.shape[1] * ncols
    tgt_count = target_points.shape[1] * nrows
    nsrc = src_count * nrows
    ntgt = tgt_count * ncols
    log_nsrc = math.log2(nsrc)
    log_ntgt = math.log2(ntgt)
    stack = -(-(6 * depth + 2 * SUB) // LANES) * LANES
    f32 = jnp.float32
    by_src = jax.ShapeDtypeStruct((src_count // LANES, LANES), f32)
    by_tgt = jax.ShapeDtypeStruct((tgt_count // LANES, LANES), f32)
    square = pltpu.VMEM((tgt_count, src_count), f32)
    wide = pltpu.VMEM((tgt_count, LANES), f32)
    row_src = pltpu.VMEM(by_src.shape, f32)
    row_tgt = pltpu.VMEM(by_tgt.shape, f32)

    def pin(value):
        return pltpu.with_memory_space_constraint(value, pltpu.VMEM)

    targets = gather_rows(target_points)
    sources = [same_block(source_points, d) for d in range(1, ncols)]
    place = jnp.stack([lax.axis_index("cols"), lax.axis_index("rows")]).astype(jnp.int32)
    bf16 = jnp.bfloat16
    piece = source_points.shape[1]
    by_piece = jax.ShapeDtypeStruct((piece // LANES, LANES), f32)
    line = jax.ShapeDtypeStruct((1, LANES), f32)
    own_norms, own_right, own_tgt, own_g0 = call(
        own_pieces_kernel,
        [
            by_piece,
            pltpu.VMEM((stack, piece), bf16),
            jax.ShapeDtypeStruct(target_points.shape, f32),
            jax.ShapeDtypeStruct((1, tgt_count), f32),
        ],
        3,
        [pltpu.VMEM(source_points.shape, f32), pltpu.SemaphoreType.DMA((3,))],
        hbm=3,
    )(
        *(
            pltpu.with_memory_space_constraint(own, pltpu.HBM)
            for own in (source_points, target_points, target_init.reshape(1, tgt_count))
        ),
    )
    own_lse, left, own_right, base, own_flag, ratios = call(
        own_scores_kernel,
        [
            by_piece,
            pltpu.VMEM((tgt_count, stack), bf16),
            pltpu.VMEM((stack, piece), bf16),
            line,
            line,
            square,
        ],
        3 + nrows,
        [
            pltpu.VMEM((stack, tgt_count), bf16),
            pltpu.VMEM((depth, tgt_count), f32),
            pltpu.VMEM((SUB, piece), f32),
        ],
        limit=16,
        smem=1,
    )(place, pin(own_right), own_g0, own_tgt, *targets)
    left = pin(left)
    lse, norms, right, flag, ratios = call(
        scores_kernel,
        [by_src, by_src, pltpu.VMEM((stack, src_count), bf16), line, square],
        7 + ncols,
        [pltpu.VMEM((SUB, src_count), f32)],
        limit=16,
        smem=1,
        aliases={7: 4},
    )(place, left, pin(own_right), own_lse, own_norms, base, own_flag, pin(ratios), *sources)
    ratios, _, phi, scale, peaks, lse = call(
        functools.partial(first_columns_kernel, log_ntgt, 6 * depth),
        [square, pltpu.VMEM((stack, src_count), bf16), by_src, by_src, by_tgt, by_tgt],
        6,
        [wide, wide, row_tgt],
        aliases={4: 0, 5: 1},
    )(left, base, flag, combine_cols(lse2, lse), pin(ratios), pin(right))
    ratios = pin(ratios)
    total, weights, shift = call(
        functools.partial(first_rows_kernel, log_nsrc),
        [by_src, by_tgt, by_tgt],
        4,
    )(ratios, scale, peaks, combine_rows(lse2, lse))
    for step in range(1, ITERS):
        last = step == ITERS - 1
        row_total = combine_cols(add_all, total)
        if last:
            f = (phi + (log_ntgt - jnp.log2(row_total))) * (1.0 / ALPHA) + norms
            other_f = swap(f, "rows", 1)
        (total,) = call(
            functools.partial(columns_kernel, float(ntgt)),
            [by_tgt],
            4,
            [row_src],
        )(ratios, scale, weights, row_total)
        if last:
            total, f, other_f = lax.optimization_barrier((total, f, other_f))
        total = combine_rows(add_all, total)
        if not last:
            (total,) = call(
                functools.partial(rows_kernel, float(nsrc)),
                [by_src],
                4,
            )(ratios, scale, weights, total)
    column = lax.broadcasted_iota(jnp.int32, f.shape, 0) // (piece // LANES)
    f = jnp.where(parity(column ^ lax.axis_index("cols")) == 0, f, other_f)
    (delta,) = call(functools.partial(finish_kernel, log_nsrc), [by_tgt], 2)(shift, total)
    delta = delta.reshape(-1, SUB, LANES).transpose(0, 2, 1).reshape(-1)
    return f.reshape(-1), target_init + delta


def solution(mesh):
    in_specs = (P(None, ("rows", "cols")), P(None, ("cols", "rows")), P("cols"))
    out_specs = (P("rows"), P("cols"))
    return jax.shard_map(body, mesh=mesh, in_specs=in_specs, out_specs=out_specs, check_vma=False)
```
